32 devices in a mesh: dp: 4 (over x, core), expert: 8 (over z, y).
Axes of the slice: x: 2, y: 2, z: 4, core: 2. Of those that a mesh axis runs over, the one named last changes fastest.
Arguments:
- tokens: bfloat16 [8192, 768], P(('dp', 'expert')), may hold values from -6 to 6
- segments: int32 [64, 128], P(('dp', 'expert')), may hold values from 0 to 3, never falling along the last dimension, each value on 1 to 64 neighbouring positions
- routes: int32 [8192, 1], P(('dp', 'expert')), may hold values from 0 to 7; in each aligned block of 128 rows (0 to 127, 128 to 255, ...) at most 20 rows name the same one
- qkv_weight: bfloat16 [768, 2304], P(('dp', 'expert')), may hold values from -0.21875 to 0.21875
- out_weight: bfloat16 [768, 768], P(('dp', 'expert')), may hold values from -1.25 to 1.25
- router_weight: bfloat16 [768, 8], P(('dp', 'expert')), may hold values from -0.15625 to 0.15625
- attn_gain: bfloat16 [768], P(('dp', 'expert')), may hold values from 0.5 to 1.5
- moe_gain: bfloat16 [768], P(('dp', 'expert')), may hold values from 0.5 to 1.5
- bias_table: bfloat16 [32, 12], replicated, may hold values from -4 to 4
- up_weight: bfloat16 [8, 768, 3072], P('expert', None, 'dp'), may hold values from -0.21875 to 0.21875
- down_weight: bfloat16 [8, 3072, 768], P('expert', 'dp'), may hold values from -0.875 to 0.875
- cotangent: bfloat16 [8192, 768], P(('dp', 'expert')), may hold values from -6 to 6
Outputs:
- mixed: bfloat16 [8192, 768], P(('dp', 'expert'))
- grad_tokens: float32 [8192, 768], P(('dp', 'expert'))
- grad_qkv: float32 [768, 2304], P(('dp', 'expert'))
- grad_out: float32 [768, 768], P(('dp', 'expert'))
- grad_router: float32 [768, 8], P(('dp', 'expert'))
- grad_attn_gain: float32 [768], P(('dp', 'expert'))
- grad_moe_gain: float32 [768], P(('dp', 'expert'))
- grad_table: float32 [32, 12], replicated
- grad_up: float32 [8, 768, 3072], P('expert', None, 'dp')
- grad_down: float32 [8, 3072, 768], P('expert', 'dp')
The draws below stay inside these ranges and needn't reach their ends.
Inputs may be any that keep to these rules, and one draw needn't show every extreme that they name: `segments`: each row holds 4 sequences in order, one of them exactly 64 tokens long. `routes`: within the 128 rows of one slab no expert is named more than 20 times, a bound that some block reaches.
All inputs are finite; a program needn't handle non-finite values.
Results may differ from the reference program's by a relative error of at most 0.015.
Values may be sent and summed in bfloat16 or wider, within the bound.
A program may use at most 128 MiB of HBM per device.

```python
import math
import jax
import jax.numpy as jnp
import numpy as np
from jax import lax

D = 768
H = 12
FF = 3072
BUCKETS = 32
MB_TOK = 128
SEGS = 4
EXPERTS = 8
CAP = 20
LONGEST = 64
SLABS = 64
TOKENS = 8192


def with_spikes(values, rng, source, target, shards_of, factor):
    owner, partner = [(jnp.arange(values.shape[axis_at]) // (values.shape[axis_at] // shards_of)).reshape([-1 if axis == axis_at else 1 for axis in range(values.ndim)]) for axis_at in (source, target)]
    chosen = jax.random.permutation(rng, shards_of)[partner]
    strong = (owner == chosen) | (owner == (partner + shards_of // 2) % shards_of)
    return jnp.where(strong, factor * values, values)


def shard_levels(own_key, extent, cuts, low, high):
    def one(dim, blocks):
        heights = jax.random.uniform(jax.random.fold_in(jax.random.fold_in(own_key, 6), dim), (blocks,), jnp.float32, low / len(cuts), high / len(cuts))
        return jnp.repeat(jnp.exp(heights), extent[dim] // blocks).reshape((-1,) + (1,) * (len(extent) - dim - 1))

    loudness = one(*cuts[0])
    for cut in cuts[1:]:
        loudness = loudness * one(*cut)
    return loudness


def split_up(number_of, total, bound, lean):
    portions = [(1 << 20) // math.isqrt(rank ** lean) + 1 for rank in range(2, number_of + 1)]
    rest, holding = total - bound - (number_of - 1), [1] * (number_of - 1)
    while rest > 0:
        movable = [i for i in range(number_of - 1) if holding[i] < bound]
        mass, budget = sum([portions[i] for i in movable]), rest
        for i in movable:
            addition = min(bound - holding[i], max(1, budget * portions[i] // mass), rest)
            holding[i] = holding[i] + addition
            rest = rest - addition
    return np.array([bound] + holding)


def ragged_sizes(stream_key, number_of, total, limit, skew):
    if number_of == 2:
        one = jax.random.randint(stream_key, (), max(1, total - limit), min(limit, total - 1) + 1)
        return jnp.stack([one, total - one])
    lengths = jnp.asarray(split_up(number_of, total, limit, skew), jnp.int32)
    pairs = (number_of - 1) // 2
    giver, receiver = lengths[1:1 + 2 * pairs:2], lengths[2:2 + 2 * pairs:2]
    slack = jnp.minimum(giver - 1, limit - receiver)
    shifted = jax.random.randint(jax.random.fold_in(stream_key, 1), (pairs,), 0, 1 << 20) % (slack + 1)
    lengths = lengths.at[1:1 + 2 * pairs:2].set(giver - shifted).at[2:2 + 2 * pairs:2].set(receiver + shifted)
    return lengths[jax.random.permutation(jax.random.fold_in(stream_key, 2), number_of)]


def deal_out(key, own, number, rows, count, top, reach, skew):
    sequence = jax.random.permutation(key, count)
    crowded, common = portions_of(count, rows * top, reach, skew, True), portions_of(count, rows * top, reach, skew, False)
    places = jnp.arange(count)

    def named(tallies, turn):
        used = int((tallies > 0).sum())
        fixed = max(1, used // 4)
        passed = fixed + (places - fixed + turn * (used - fixed)) % max(1, count - fixed)
        return jnp.zeros((count,), jnp.int32).at[sequence[jnp.where(places < fixed, places, passed)]].set(jnp.asarray(tallies, jnp.int32))

    tallies = jnp.where(number % 4 == 0, named(crowded, number // 4), named(common, number - number // 4 - 1))
    mixed = jax.random.permutation(jax.random.fold_in(own, 3), count)
    giver, sink = mixed[0:count // 2 * 2:2], mixed[1:count // 2 * 2:2]
    slack = jnp.minimum(tallies[giver] - 1, reach - tallies[sink]) // 2
    slack = jnp.where((giver == sequence[0]) | (sink == sequence[0]) | (tallies[sink] == 0), 0, jnp.maximum(slack, 0))
    passed = jax.random.randint(jax.random.fold_in(own, 4), (count // 2,), 0, 1 << 20) % (slack + 1)
    tallies = tallies.at[giver].add(-passed).at[sink].add(passed)
    items = jnp.searchsorted(jnp.cumsum(tallies), jnp.arange(rows * top), side="right").astype(jnp.int32)
    listing = items.reshape(top, rows).T
    listing = listing[jax.random.permutation(jax.random.fold_in(own, 1), rows)]
    turn = jax.random.randint(jax.random.fold_in(own, 2), (rows, 1), 0, top)
    return jnp.take_along_axis(listing, (jnp.arange(top)[None, :] + turn) % top, axis=1)


def portions_of(count, total, most, slope, full):
    weights = [(1 << 20) // math.isqrt(grade ** slope) + 1 for grade in range(1, count + 1)]
    largest = most if full else min(most, max(-(-total // count), total * weights[0] // sum(weights)))
    least = 1 if total - largest >= count - 1 else 0
    given, surplus = [largest] + [least] * (count - 1), total - largest - least * (count - 1)
    while surplus > 0:
        candidates = [i for i in range(1, count) if given[i] < largest] or [i for i in range(1, count) if given[i] < most]
        mass, remaining = sum([weights[i] for i in candidates]), surplus
        for i in candidates:
            extra = min(most - given[i], max(1, remaining * weights[i] // mass), surplus)
            given[i] = given[i] + extra
            surplus = surplus - extra
    return np.array(given)


def normal_values(rng, extent, deviation, bound, shards=(), kind=jnp.bfloat16):
    level = shard_levels(rng, extent, shards, -0.22, 0.18) if shards else 1.0
    drawn = jax.random.normal(rng, extent, jnp.float32) * deviation * level
    return jnp.minimum(jnp.maximum(drawn, -bound), bound).astype(kind)


def bell_draw_with(key, dims, scale, bound, split, heavy, kind=jnp.bfloat16):
    array = scale * jax.random.normal(key, dims, jnp.float32)
    if split:
        array = array * shard_levels(key, dims, split, -0.22, 0.18)
    return jnp.clip(with_spikes(array, jax.random.fold_in(key, 3), *heavy), -bound, bound).astype(kind)


def setup_inputs(seed: int = 0) -> dict:
    arg_keys = jax.random.split(jax.random.key(seed), 13)
    tokens = bell_draw_with(arg_keys[0], (TOKENS, D), 1.0, 6.0, ((0, 32),), (0, 1, 32, 2.75))
    segments = jax.vmap(lambda own: jnp.searchsorted(jnp.cumsum(ragged_sizes(own, SEGS, MB_TOK, LONGEST, 1)), jnp.arange(MB_TOK), side="right"))(jax.random.split(arg_keys[1], SLABS)).reshape((SLABS, MB_TOK)).astype(jnp.int32)
    routes_keys = jax.random.split(jax.random.fold_in(arg_keys[2], 1), TOKENS // MB_TOK)
    routes_turns = jax.random.permutation(jax.random.fold_in(arg_keys[2], 3), TOKENS // MB_TOK)
    routes = jax.vmap(lambda own, number: deal_out(jax.random.fold_in(arg_keys[2], 2), own, number, MB_TOK, EXPERTS, 1, CAP, 2))(routes_keys, routes_turns).reshape((TOKENS, 1))
    qkv_weight = normal_values(arg_keys[3], (D, 3 * D), D ** -0.5, 0.21875, ((0, 32),))
    out_weight = normal_values(arg_keys[4], (D, D), (D // 32) ** -0.5, 1.25, ((0, 32),))
    router_weight = normal_values(arg_keys[5], (D, EXPERTS), (2 * D) ** -0.5, 0.15625, ((0, 32),))
    attn_gain = jnp.clip(1.0 + 0.1 * jax.random.normal(arg_keys[6], (D,), jnp.float32), 0.5, 1.5).astype(jnp.bfloat16)
    moe_gain = jnp.clip(1.0 + 0.1 * jax.random.normal(arg_keys[7], (D,), jnp.float32), 0.5, 1.5).astype(jnp.bfloat16)
    bias_table = normal_values(arg_keys[8], (BUCKETS, H), 1.0, 4.0)
    up_weight = normal_values(arg_keys[9], (EXPERTS, D, FF), D ** -0.5, 0.21875, ((0, 8), (2, 4)))
    down_weight = normal_values(arg_keys[10], (EXPERTS, FF, D), (max(1, FF // (EXPERTS * EXPERTS))) ** -0.5, 0.875, ((0, 8), (1, 4)))
    cotangent = normal_values(arg_keys[11], (TOKENS, D), 1.0, 6.0, ((0, 32),))
    return dict(tokens=tokens, segments=segments, routes=routes, qkv_weight=qkv_weight, out_weight=out_weight, router_weight=router_weight, attn_gain=attn_gain, moe_gain=moe_gain, bias_table=bias_table, up_weight=up_weight, down_weight=down_weight, cotangent=cotangent)


EPS = 1e-06
MASKED = -1e+30

@jax.custom_vjp
def low(v):
    return lax.optimization_barrier(v.astype(jnp.bfloat16)).astype(jnp.float32)

@jax.custom_vjp
def low_back(v):
    return v

def low_keep(v):
    return (low(v), None)

def low_pass(kept, grad):
    return (grad,)

def back_keep(v):
    return (v, None)

def back_low(kept, grad):
    return (low(grad),)
low.defvjp(low_keep, low_pass)
low_back.defvjp(back_keep, back_low)

def bucket_onehot(length, buckets):
    half_count = buckets // 2
    exact_count = half_count // 2
    offsets = np.arange(length)[None, :] - np.arange(length)[:, None]
    distance = np.abs(offsets)
    scaled = np.log(np.maximum(distance, 1) / exact_count) / np.log(128.0 / exact_count) * (half_count - exact_count)
    far_bucket = np.minimum(exact_count + np.floor(scaled).astype(np.int32), half_count - 1)
    bucket = np.where(distance < exact_count, distance, far_bucket) + np.where(offsets > 0, half_count, 0)
    return (bucket[:, :, None] == np.arange(buckets)[None, None, :]).astype(np.float32)

def exact_dot(left, right):
    return jnp.dot(left, right, precision=lax.Precision.HIGHEST)

def rms_scale(values, gain_vec):
    return values * lax.rsqrt(lax.optimization_barrier(jnp.mean(values * values, axis=-1, keepdims=True)) + EPS) * gain_vec

def attention_group(inputs, same_doc, rel_bias, gain_vec, w_qkv, w_out):
    group_count, length, model_width = inputs.shape
    head_count = rel_bias.shape[0]
    head_size = model_width // head_count
    normed = low(rms_scale(inputs, gain_vec))
    packed = jnp.einsum('gld,de->gle', normed, w_qkv, precision=lax.Precision.HIGHEST)
    packed = low_back(low(packed)).reshape(group_count, length, 3, head_count, head_size)
    query_rows = packed[:, :, 0]
    key_rows = packed[:, :, 1]
    value_rows = packed[:, :, 2]
    scores = jnp.einsum('gqhd,gkhd->ghqk', query_rows, key_rows, precision=lax.Precision.HIGHEST)
    scores = low_back(scores * head_size ** (-0.5))
    scores = jnp.where(same_doc[:, None], scores + rel_bias[None], MASKED)
    attn_probs = jax.nn.softmax(scores, axis=-1)
    attended = jnp.einsum('ghqk,gkhd->gqhd', low(attn_probs), value_rows, precision=lax.Precision.HIGHEST)
    attended = low_back(low(attended)).reshape(group_count, length, model_width)
    branch = low_back(jnp.einsum('gle,ed->gld', attended, w_out, precision=lax.Precision.HIGHEST))
    return inputs + branch

def expert_rows(rows_in, w_up, w_down):
    hidden = low_back(exact_dot(rows_in, w_up))
    activation = low(jax.nn.gelu(hidden, approximate=True))
    return low_back(low(exact_dot(activation, w_down)))

def reference(tokens, segments, routes, qkv_weight, out_weight, router_weight, attn_gain, moe_gain, bias_table, up_weight, down_weight, cotangent):
    model_width = tokens.shape[1]
    group_size = math.gcd(SLABS, max(1, 4096 // MB_TOK))
    same_doc = (segments[:, :, None] == segments[:, None, :]).reshape(SLABS // group_size, group_size, MB_TOK, MB_TOK)
    route_ids = routes.reshape(SLABS, MB_TOK)
    route_hot = (route_ids[:, :, None] == jnp.arange(EXPERTS, dtype=jnp.int32)[None, None, :]).astype(jnp.int32)
    slot_index = lax.optimization_barrier(jnp.sum(route_hot * (jnp.cumsum(route_hot, axis=1) - 1), axis=2))
    position = route_ids * CAP + slot_index
    place_hot = (jnp.arange(EXPERTS * CAP, dtype=jnp.int32)[None, :, None] == position[:, None, :]).astype(jnp.float32)
    token_hot = route_hot.reshape(TOKENS, EXPERTS).astype(jnp.float32)
    onehot = jnp.asarray(bucket_onehot(MB_TOK, BUCKETS)).astype(jnp.float32)

    def forward(inputs, w_qkv, w_out, w_router, gain_one, gain_two, table, w_up, w_down):
        rel_bias = jnp.einsum('qkb,bh->hqk', onehot, table, precision=lax.Precision.HIGHEST)

        def attend(pieces):
            return attention_group(pieces[0], pieces[1], rel_bias, gain_one, w_qkv, w_out)
        grouped = inputs.reshape(SLABS // group_size, group_size, MB_TOK, model_width)
        after_attn = lax.map(jax.checkpoint(attend), (grouped, same_doc)).reshape(TOKENS, model_width)
        normed_two = low(rms_scale(after_attn, gain_two))
        logits = low_back(exact_dot(normed_two, w_router))
        router_probs = jax.nn.softmax(logits, axis=-1)
        gate_prob = lax.optimization_barrier(jnp.sum(router_probs * token_hot, axis=-1, keepdims=True))
        slab_rows = normed_two.reshape(SLABS, MB_TOK, model_width)
        sent_rows = jnp.einsum('sck,skd->scd', place_hot, slab_rows, precision=lax.Precision.HIGHEST)
        sent_rows = low_back(sent_rows)
        sent_rows = sent_rows.reshape(SLABS, EXPERTS, CAP, model_width).transpose(1, 0, 2, 3)
        sent_rows = sent_rows.reshape(EXPERTS, SLABS * CAP, model_width)

        def run_expert(pieces):
            return expert_rows(pieces[0], pieces[1], pieces[2])
        back_rows = lax.map(jax.checkpoint(run_expert), (sent_rows, w_up, w_down))
        back_rows = back_rows.reshape(EXPERTS, SLABS, CAP, model_width).transpose(1, 0, 2, 3)
        back_rows = back_rows.reshape(SLABS, EXPERTS * CAP, model_width)
        returned = jnp.einsum('sck,scd->skd', place_hot, back_rows, precision=lax.Precision.HIGHEST)
        return after_attn + gate_prob * returned.reshape(TOKENS, model_width)
    floats = (tokens.astype(jnp.float32), qkv_weight.astype(jnp.float32), out_weight.astype(jnp.float32), router_weight.astype(jnp.float32), attn_gain.astype(jnp.float32), moe_gain.astype(jnp.float32), bias_table.astype(jnp.float32), up_weight.astype(jnp.float32), down_weight.astype(jnp.float32))
    result, pullback = jax.vjp(forward, *floats)
    grads = pullback(cotangent.astype(jnp.float32))
    return (result.astype(jnp.bfloat16), grads[0], grads[1], grads[2], grads[3], grads[4], grads[5], grads[6], grads[7], grads[8])
```

```python
import jax
import jax.numpy as jnp
import numpy as np
from jax import lax
from jax.sharding import PartitionSpec as P

EPS = 1e-06
MASKED = -1e30


def bucket_onehot(length, buckets):
    half_count = buckets // 2
    exact_count = half_count // 2
    offsets = np.arange(length)[None, :] - np.arange(length)[:, None]
    distance = np.abs(offsets)
    scaled = (
        np.log(np.maximum(distance, 1) / exact_count)
        / np.log(128.0 / exact_count)
        * (half_count - exact_count)
    )
    far_bucket = np.minimum(exact_count + np.floor(scaled).astype(np.int32), half_count - 1)
    bucket = np.where(distance < exact_count, distance, far_bucket) + np.where(
        offsets > 0, half_count, 0
    )
    return (bucket[:, :, None] == np.arange(buckets)[None, None, :]).astype(np.float32)


def rms_scale(values, gain_vec):
    return values * lax.rsqrt(jnp.mean(values * values, axis=-1, keepdims=True) + EPS) * gain_vec


def gelu_tanh(values):
    return jax.nn.gelu(values, approximate=True)


def left_dot(left, right):
    return lax.dot_general(
        left, right, (((0,), (0,)), ((), ())), preferred_element_type=jnp.float32
    )


def right_dot(left, right):
    return lax.dot_general(
        left, right, (((1,), (1,)), ((), ())), preferred_element_type=jnp.float32
    )


def shards(
    tokens,
    segments,
    routes,
    qkv_weight,
    out_weight,
    router_weight,
    attn_gain,
    moe_gain,
    bias_table,
    up_weight,
    down_weight,
    cotangent,
):
    both = ("dp", "expert")
    micro_count, length = segments.shape
    rows, model_width = tokens.shape
    buckets, head_count = bias_table.shape
    head_size = model_width // head_count
    score_scale = head_size ** (-0.5)
    experts = router_weight.shape[1]
    capacity = max(2, (5 * length + 4 * experts - 1) // (4 * experts))
    packed_width = qkv_weight.shape[1]
    side_pad = (-(experts + 2)) % 128

    first_part = jnp.concatenate(
        [
            qkv_weight,
            router_weight,
            attn_gain[:, None],
            moe_gain[:, None],
            jnp.zeros((qkv_weight.shape[0], side_pad), jnp.bfloat16),
        ],
        axis=1,
    )
    first_whole = lax.all_gather(first_part, both, axis=0, tiled=True)
    w_out = lax.all_gather(out_weight, both, axis=0, tiled=True)
    w_qkv = first_whole[:, :packed_width]
    side = first_whole[:, packed_width:]
    w_router = side[:, :experts]
    gain_one = side[:, experts].astype(jnp.float32)
    gain_two = side[:, experts + 1].astype(jnp.float32)
    up_mat, down_mat = (up_weight[0], down_weight[0])

    bucket_hot = bucket_onehot(length, buckets)
    flat_hot = jnp.asarray(bucket_hot.reshape(length * length, buckets).astype(jnp.bfloat16))
    rel_bias = jnp.dot(flat_hot, bias_table, preferred_element_type=jnp.float32)
    rel_bias = rel_bias.reshape(length, length, head_count).transpose(2, 0, 1)

    inputs = tokens.astype(jnp.float32)
    upstream = cotangent.astype(jnp.float32)
    same_doc = segments[:, :, None] == segments[:, None, :]
    route_ids = routes[:, 0]
    route_hot = (route_ids[:, None] == jnp.arange(experts, dtype=jnp.int32)[None, :]).astype(
        jnp.float32
    )
    earlier = (
        (np.arange(rows)[:, None] > np.arange(rows)[None, :])
        & (np.arange(rows)[:, None] // length == np.arange(rows)[None, :] // length)
    ).astype(np.float32)
    same_route = route_ids[:, None] == route_ids[None, :]
    slot_index = jnp.sum(jnp.where(same_route, jnp.asarray(earlier), 0.0), axis=1).astype(jnp.int32)
    slab_index = jnp.arange(rows, dtype=jnp.int32) // length
    position = (route_ids * micro_count + slab_index) * capacity + slot_index
    slots = experts * micro_count * capacity
    dispatch = (jnp.arange(slots, dtype=jnp.int32)[:, None] == position[None, :]).astype(
        jnp.bfloat16
    )

    normed_one = rms_scale(inputs, gain_one).astype(jnp.bfloat16)
    packed = jnp.dot(normed_one, w_qkv, preferred_element_type=jnp.float32).astype(jnp.bfloat16)
    packed = packed.reshape(micro_count, length, 3, head_count, head_size)
    query_rows, key_rows, value_rows = (packed[:, :, 0], packed[:, :, 1], packed[:, :, 2])
    scores = (
        jnp.einsum("bqhd,bkhd->bhqk", query_rows, key_rows, preferred_element_type=jnp.float32)
        * score_scale
    )
    scores = jnp.where(same_doc[:, None], scores + rel_bias[None], MASKED)
    expo = jnp.exp(scores - jnp.max(scores, axis=-1, keepdims=True))
    attn_probs = expo / jnp.sum(expo, axis=-1, keepdims=True)
    probs_low = attn_probs.astype(jnp.bfloat16)
    attended = (
        jnp.einsum("bhqk,bkhd->bqhd", probs_low, value_rows, preferred_element_type=jnp.float32)
        .astype(jnp.bfloat16)
        .reshape(rows, model_width)
    )
    after_attn = inputs + jnp.dot(attended, w_out, preferred_element_type=jnp.float32)
    normed_two = rms_scale(after_attn, gain_two).astype(jnp.bfloat16)
    logits = jnp.dot(normed_two, w_router, preferred_element_type=jnp.float32)
    router_probs = jax.nn.softmax(logits, axis=-1)
    gate_prob = jnp.sum(router_probs * route_hot, axis=1, keepdims=True)
    grad_token_out = (gate_prob * upstream).astype(jnp.bfloat16)

    sent = jnp.dot(
        dispatch,
        jnp.concatenate([normed_two, grad_token_out], axis=1),
        preferred_element_type=jnp.float32,
    ).astype(jnp.bfloat16)
    received = lax.all_to_all(
        sent.reshape(experts, micro_count * capacity, 2 * model_width),
        "expert",
        split_axis=0,
        concat_axis=0,
        tiled=True,
    ).reshape(slots, 2 * model_width)
    expert_rows = lax.all_gather(received, "dp", axis=0, tiled=True)
    expert_in, grad_expert_out = (expert_rows[:, :model_width], expert_rows[:, model_width:])
    hidden = jnp.dot(expert_in, up_mat, preferred_element_type=jnp.float32)
    act, act_back = jax.vjp(gelu_tanh, hidden)
    act_low = act.astype(jnp.bfloat16)
    grad_activation = right_dot(grad_expert_out, down_mat)
    grad_hidden = act_back(grad_activation)[0].astype(jnp.bfloat16)
    results = jnp.concatenate(
        [
            jnp.dot(act_low, down_mat, preferred_element_type=jnp.float32).astype(jnp.bfloat16),
            right_dot(grad_hidden, up_mat).astype(jnp.bfloat16),
        ],
        axis=1,
    )
    results = lax.psum_scatter(results, "dp", scatter_dimension=0, tiled=True)
    returned = lax.all_to_all(
        results.reshape(experts, micro_count * capacity, 2 * model_width),
        "expert",
        split_axis=0,
        concat_axis=0,
        tiled=True,
    ).reshape(slots, 2 * model_width)
    acc_up = left_dot(expert_in, grad_hidden)
    acc_down = left_dot(act_low, grad_expert_out)
    back = left_dot(dispatch, returned)
    combined, grad_normed_two = (back[:, :model_width], back[:, model_width:])
    mixed = (after_attn + gate_prob * combined).astype(jnp.bfloat16)
    grad_gate = jnp.sum(upstream * combined, axis=1, keepdims=True)
    grad_logits = (router_probs * (route_hot - gate_prob) * grad_gate).astype(jnp.bfloat16)
    grad_normed_two = grad_normed_two + right_dot(grad_logits, w_router)
    grad_after_norm, grad_gain_two = jax.vjp(rms_scale, after_attn, gain_two)[1](grad_normed_two)
    grad_after = upstream + grad_after_norm
    grad_branch = grad_after.astype(jnp.bfloat16)

    acc_out = left_dot(attended, grad_branch)
    acc_router = left_dot(normed_two, grad_logits)
    out_share = lax.psum_scatter(
        jnp.concatenate(
            [
                acc_out,
                acc_router,
                grad_gain_two[:, None],
                jnp.zeros((model_width, (-(experts + 1)) % 128), jnp.float32),
            ],
            axis=1,
        ).astype(jnp.bfloat16),
        both,
        scatter_dimension=0,
        tiled=True,
    ).astype(jnp.float32)

    grad_attended = (
        right_dot(grad_branch, w_out)
        .astype(jnp.bfloat16)
        .reshape(micro_count, length, head_count, head_size)
    )
    grad_value = jnp.einsum(
        "bhqk,bqhd->bkhd", probs_low, grad_attended, preferred_element_type=jnp.float32
    )
    grad_probs = jnp.einsum(
        "bqhd,bkhd->bhqk", grad_attended, value_rows, preferred_element_type=jnp.float32
    )
    grad_scores = attn_probs * (
        grad_probs - jnp.sum(attn_probs * grad_probs, axis=-1, keepdims=True)
    )
    scores_low = grad_scores.astype(jnp.bfloat16)
    grad_query = (
        jnp.einsum("bhqk,bkhd->bqhd", scores_low, key_rows, preferred_element_type=jnp.float32)
        * score_scale
    )
    grad_key = (
        jnp.einsum("bhqk,bqhd->bkhd", scores_low, query_rows, preferred_element_type=jnp.float32)
        * score_scale
    )
    grad_packed = (
        jnp.stack([grad_query, grad_key, grad_value], axis=2)
        .reshape(rows, packed_width)
        .astype(jnp.bfloat16)
    )
    grad_normed_one = right_dot(grad_packed, w_qkv)
    grad_input_norm, grad_gain_one = jax.vjp(rms_scale, inputs, gain_one)[1](grad_normed_one)
    grad_tokens = grad_after + grad_input_norm
    acc_qkv = left_dot(normed_one, grad_packed)
    qkv_share = lax.psum_scatter(
        jnp.concatenate(
            [
                acc_qkv.astype(jnp.bfloat16),
                grad_gain_one[:, None].astype(jnp.bfloat16),
                jnp.zeros((model_width, 127), jnp.bfloat16),
            ],
            axis=1,
        ),
        both,
        scatter_dimension=0,
        tiled=True,
    ).astype(jnp.float32)

    flat_scores = jnp.sum(grad_scores, axis=0).reshape(head_count, length * length)
    high = flat_scores.astype(jnp.bfloat16)
    low = (flat_scores - high.astype(jnp.float32)).astype(jnp.bfloat16)
    table_parts = jnp.dot(
        jnp.concatenate([high, low], axis=0), flat_hot, preferred_element_type=jnp.float32
    )
    acc_table = (table_parts[:head_count] + table_parts[head_count:]).T
    table_total = lax.psum(acc_table, both)
    return (
        mixed,
        grad_tokens,
        qkv_share[:, :packed_width],
        out_share[:, :model_width],
        out_share[:, model_width : model_width + experts],
        qkv_share[:, packed_width],
        out_share[:, model_width + experts],
        table_total,
        acc_up[None],
        acc_down[None],
    )


def solution(mesh):
    in_specs = (
        P(("dp", "expert"), None),
        P(("dp", "expert"), None),
        P(("dp", "expert"), None),
        P(("dp", "expert"), None),
        P(("dp", "expert"), None),
        P(("dp", "expert"), None),
        P(("dp", "expert")),
        P(("dp", "expert")),
        P(),
        P("expert", None, "dp"),
        P("expert", "dp", None),
        P(("dp", "expert"), None),
    )
    out_specs = (
        P(("dp", "expert"), None),
        P(("dp", "expert"), None),
        P(("dp", "expert"), None),
        P(("dp", "expert"), None),
        P(("dp", "expert"), None),
        P(("dp", "expert")),
        P(("dp", "expert")),
        P(),
        P("expert", None, "dp"),
        P("expert", "dp", None),
    )
    return jax.shard_map(shards, mesh=mesh, in_specs=in_specs, out_specs=out_specs, check_vma=False)
```

```python
import jax
import jax.numpy as jnp
import numpy as np
from jax import lax
from jax.sharding import PartitionSpec as P

EPS = 1e-06
MASKED = -1e30


def bucket_onehot(length, buckets):
    half_count = buckets // 2
    exact_count = half_count // 2
    offsets = np.arange(length)[None, :] - np.arange(length)[:, None]
    distance = np.abs(offsets)
    scaled = (
        np.log(np.maximum(distance, 1) / exact_count)
        / np.log(128.0 / exact_count)
        * (half_count - exact_count)
    )
    far_bucket = np.minimum(exact_count + np.floor(scaled).astype(np.int32), half_count - 1)
    bucket = np.where(distance < exact_count, distance, far_bucket) + np.where(
        offsets > 0, half_count, 0
    )
    return (bucket[:, :, None] == np.arange(buckets)[None, None, :]).astype(np.float32)


def rms_scale(values, gain_vec):
    return values * lax.rsqrt(jnp.mean(values * values, axis=-1, keepdims=True) + EPS) * gain_vec


def gelu_tanh(values):
    return jax.nn.gelu(values, approximate=True)


def left_dot(left, right):
    return lax.dot_general(
        left, right, (((0,), (0,)), ((), ())), preferred_element_type=jnp.float32
    )


def right_dot(left, right):
    return lax.dot_general(
        left, right, (((1,), (1,)), ((), ())), preferred_element_type=jnp.float32
    )


def two_terms(values):
    high = lax.reduce_precision(values, exponent_bits=8, mantissa_bits=7)
    return high.astype(jnp.bfloat16), (values - high).astype(jnp.bfloat16)


def shards(
    tokens,
    segments,
    routes,
    qkv_weight,
    out_weight,
    router_weight,
    attn_gain,
    moe_gain,
    bias_table,
    up_weight,
    down_weight,
    cotangent,
):
    micro_count, length = segments.shape
    rows, model_width = tokens.shape
    buckets, head_count = bias_table.shape
    head_size = model_width // head_count
    score_scale = head_size ** (-0.5)
    experts = router_weight.shape[1]
    capacity = max(2, (5 * length + 4 * experts - 1) // (4 * experts))
    packed_width = qkv_weight.shape[1]
    side_pad = (-(experts + 2)) % 128

    first_part = jnp.concatenate(
        [
            qkv_weight,
            router_weight,
            attn_gain[:, None],
            moe_gain[:, None],
            jnp.zeros((qkv_weight.shape[0], side_pad), jnp.bfloat16),
        ],
        axis=1,
    )
    near = lax.all_gather(
        jnp.concatenate([first_part, out_weight], axis=1), "expert", axis=0, tiled=True
    )
    first_width = first_part.shape[1]
    first_whole = lax.all_gather(near[:, :first_width], "dp", axis=0, tiled=True)
    w_out = lax.all_gather(near[:, first_width:], "dp", axis=0, tiled=True)
    w_qkv = first_whole[:, :packed_width]
    side = first_whole[:, packed_width:]
    w_router = side[:, :experts]
    gain_one = side[:, experts].astype(jnp.float32)
    gain_two = side[:, experts + 1].astype(jnp.float32)
    up_mat, down_mat = (up_weight[0], down_weight[0])

    bucket_hot = bucket_onehot(length, buckets)
    flat_hot = jnp.asarray(bucket_hot.reshape(length * length, buckets).astype(jnp.bfloat16))
    rel_bias = jnp.dot(flat_hot, bias_table, preferred_element_type=jnp.float32)
    rel_bias = rel_bias.reshape(length, length, head_count).transpose(2, 0, 1)

    inputs = tokens.astype(jnp.float32)
    upstream = cotangent.astype(jnp.float32)
    same_doc = segments[:, :, None] == segments[:, None, :]
    route_ids = routes[:, 0]
    route_hot = (route_ids[:, None] == jnp.arange(experts, dtype=jnp.int32)[None, :]).astype(
        jnp.float32
    )
    earlier = (
        (np.arange(rows)[:, None] > np.arange(rows)[None, :])
        & (np.arange(rows)[:, None] // length == np.arange(rows)[None, :] // length)
    ).astype(np.float32)
    same_route = route_ids[:, None] == route_ids[None, :]
    slot_index = jnp.sum(jnp.where(same_route, jnp.asarray(earlier), 0.0), axis=1).astype(jnp.int32)
    slab_index = jnp.arange(rows, dtype=jnp.int32) // length
    position = (route_ids * micro_count + slab_index) * capacity + slot_index
    slots = experts * micro_count * capacity
    dispatch = (jnp.arange(slots, dtype=jnp.int32)[:, None] == position[None, :]).astype(
        jnp.bfloat16
    )

    normed_one = rms_scale(inputs, gain_one).astype(jnp.bfloat16)
    packed = jnp.dot(normed_one, w_qkv, preferred_element_type=jnp.float32).astype(jnp.bfloat16)
    packed = packed.reshape(micro_count, length, 3, head_count, head_size)
    query_rows, key_rows, value_rows = (packed[:, :, 0], packed[:, :, 1], packed[:, :, 2])
    scores = (
        jnp.einsum("bqhd,bkhd->bhqk", query_rows, key_rows, preferred_element_type=jnp.float32)
        * score_scale
    )
    scores = jnp.where(same_doc[:, None], scores + rel_bias[None], MASKED)
    expo = jnp.exp(scores - jnp.max(scores, axis=-1, keepdims=True))
    attn_probs = expo / jnp.sum(expo, axis=-1, keepdims=True)
    probs_low = attn_probs.astype(jnp.bfloat16)
    attended = (
        jnp.einsum("bhqk,bkhd->bqhd", probs_low, value_rows, preferred_element_type=jnp.float32)
        .astype(jnp.bfloat16)
        .reshape(rows, model_width)
    )
    after_attn = inputs + jnp.dot(attended, w_out, preferred_element_type=jnp.float32)
    normed_two = rms_scale(after_attn, gain_two).astype(jnp.bfloat16)
    logits = jnp.dot(normed_two, w_router, preferred_element_type=jnp.float32)
    router_probs = jax.nn.softmax(logits, axis=-1)
    gate_prob = jnp.sum(router_probs * route_hot, axis=1, keepdims=True)
    grad_token_out = (gate_prob * upstream).astype(jnp.bfloat16)

    sent = jnp.dot(
        dispatch,
        jnp.concatenate([normed_two, grad_token_out], axis=1),
        preferred_element_type=jnp.float32,
    ).astype(jnp.bfloat16)
    received = lax.all_to_all(
        sent.reshape(experts, micro_count * capacity, 2 * model_width),
        "expert",
        split_axis=0,
        concat_axis=0,
        tiled=True,
    ).reshape(slots, 2 * model_width)
    expert_rows = lax.all_gather(received, "dp", axis=0, tiled=True)
    expert_in, grad_expert_out = (expert_rows[:, :model_width], expert_rows[:, model_width:])
    hidden = jnp.dot(expert_in, up_mat, preferred_element_type=jnp.float32)
    act, act_back = jax.vjp(gelu_tanh, hidden)
    act_low = act.astype(jnp.bfloat16)
    grad_activation = right_dot(grad_expert_out, down_mat)
    grad_hidden = act_back(grad_activation)[0].astype(jnp.bfloat16)
    results = jnp.concatenate(
        [
            jnp.dot(act_low, down_mat, preferred_element_type=jnp.float32).astype(jnp.bfloat16),
            right_dot(grad_hidden, up_mat).astype(jnp.bfloat16),
        ],
        axis=1,
    )
    results = lax.psum_scatter(results, "dp", scatter_dimension=0, tiled=True)
    returned = lax.all_to_all(
        results.reshape(experts, micro_count * capacity, 2 * model_width),
        "expert",
        split_axis=0,
        concat_axis=0,
        tiled=True,
    ).reshape(slots, 2 * model_width)
    acc_up = left_dot(expert_in, grad_hidden)
    acc_down = left_dot(act_low, grad_expert_out)
    back = left_dot(dispatch, returned)
    combined, grad_normed_two = (back[:, :model_width], back[:, model_width:])
    mixed = (after_attn + gate_prob * combined).astype(jnp.bfloat16)
    grad_gate = jnp.sum(upstream * combined, axis=1, keepdims=True)
    grad_logits = (router_probs * (route_hot - gate_prob) * grad_gate).astype(jnp.bfloat16)
    grad_normed_two = grad_normed_two + right_dot(grad_logits, w_router)
    grad_after_norm, grad_gain_two = jax.vjp(rms_scale, after_attn, gain_two)[1](grad_normed_two)
    grad_after = upstream + grad_after_norm
    grad_branch = grad_after.astype(jnp.bfloat16)

    acc_out = left_dot(attended, grad_branch)
    acc_router = left_dot(grad_logits, normed_two)
    out_near = lax.psum_scatter(
        acc_out.astype(jnp.bfloat16), "dp", scatter_dimension=0, tiled=True
    )

    grad_attended = (
        right_dot(grad_branch, w_out)
        .astype(jnp.bfloat16)
        .reshape(micro_count, length, head_count, head_size)
    )
    grad_value = jnp.einsum(
        "bhqk,bqhd->bkhd", probs_low, grad_attended, preferred_element_type=jnp.float32
    )
    grad_probs = jnp.einsum(
        "bqhd,bkhd->bhqk", grad_attended, value_rows, preferred_element_type=jnp.float32
    )
    grad_scores = attn_probs * (
        grad_probs - jnp.sum(attn_probs * grad_probs, axis=-1, keepdims=True)
    )
    scores_low = grad_scores.astype(jnp.bfloat16)
    grad_query = (
        jnp.einsum("bhqk,bkhd->bqhd", scores_low, key_rows, preferred_element_type=jnp.float32)
        * score_scale
    )
    grad_key = (
        jnp.einsum("bhqk,bqhd->bkhd", scores_low, query_rows, preferred_element_type=jnp.float32)
        * score_scale
    )
    grad_packed = (
        jnp.stack([grad_query, grad_key, grad_value], axis=2)
        .reshape(rows, packed_width)
        .astype(jnp.bfloat16)
    )
    grad_normed_one = right_dot(grad_packed, w_qkv)
    grad_input_norm, grad_gain_one = jax.vjp(rms_scale, inputs, gain_one)[1](grad_normed_one)
    grad_tokens = grad_after + grad_input_norm
    acc_qkv = left_dot(normed_one, grad_packed)
    qkv_sum, table_scores = lax.optimization_barrier(
        (acc_qkv.astype(jnp.bfloat16), jnp.sum(grad_scores, axis=0))
    )
    qkv_near = lax.psum_scatter(qkv_sum, "dp", scatter_dimension=0, tiled=True)

    high, low = two_terms(table_scores.reshape(head_count, length * length))
    table_parts = jnp.dot(
        jnp.concatenate([high, low], axis=0), flat_hot, preferred_element_type=jnp.float32
    )
    acc_table = (table_parts[:head_count] + table_parts[head_count:]).reshape(-1)

    shard_rows = qkv_weight.shape[0]
    experts_axis = near.shape[0] // shard_rows
    small_rows = experts + 3
    small = jnp.concatenate(
        [
            acc_router,
            grad_gain_one[None],
            grad_gain_two[None],
            jnp.pad(acc_table, (0, model_width - acc_table.shape[0]))[None],
            jnp.zeros(((-small_rows) % 8, model_width), jnp.float32),
        ],
        axis=0,
    )
    small = jnp.sum(lax.all_gather(small, "dp", axis=0, tiled=False), axis=0)
    mine = lax.dynamic_slice_in_dim(
        small[: experts + 2], lax.axis_index("dp") * near.shape[0], near.shape[0], axis=1
    )
    mine = mine.T.reshape(experts_axis, shard_rows, experts + 2)
    table_size = buckets * head_count
    table_columns = -(-table_size // shard_rows)
    table_block = jnp.pad(
        small[experts + 2, :table_size], (0, table_columns * shard_rows - table_size)
    ).reshape(1, shard_rows, table_columns)
    extra = jnp.concatenate(
        [mine, jnp.broadcast_to(table_block, (experts_axis, shard_rows, table_columns))], axis=2
    )
    extra_width = extra.shape[2]
    extra_high, extra_low = two_terms(extra)
    share = jnp.concatenate(
        [
            qkv_near.reshape(experts_axis, shard_rows, packed_width),
            out_near.reshape(experts_axis, shard_rows, model_width),
            extra_high,
            extra_low,
            jnp.zeros((experts_axis, shard_rows, (-2 * extra_width) % 128), jnp.bfloat16),
        ],
        axis=2,
    )
    share = lax.all_to_all(share, "expert", split_axis=0, concat_axis=0, tiled=True)
    share = jnp.sum(share.astype(jnp.float32), axis=0)
    dense_width = packed_width + model_width
    extra_sum = (
        share[:, dense_width : dense_width + extra_width]
        + share[:, dense_width + extra_width : dense_width + 2 * extra_width]
    )
    table_total = (
        extra_sum[:, experts + 2 :].reshape(-1)[:table_size].reshape(head_count, buckets).T
    )
    return (
        mixed,
        grad_tokens,
        share[:, :packed_width],
        share[:, packed_width:dense_width],
        extra_sum[:, :experts],
        extra_sum[:, experts],
        extra_sum[:, experts + 1],
        table_total,
        acc_up[None],
        acc_down[None],
    )


def solution(mesh):
    in_specs = (
        P(("dp", "expert"), None),
        P(("dp", "expert"), None),
        P(("dp", "expert"), None),
        P(("dp", "expert"), None),
        P(("dp", "expert"), None),
        P(("dp", "expert"), None),
        P(("dp", "expert")),
        P(("dp", "expert")),
        P(),
        P("expert", None, "dp"),
        P("expert", "dp", None),
        P(("dp", "expert"), None),
    )
    out_specs = (
        P(("dp", "expert"), None),
        P(("dp", "expert"), None),
        P(("dp", "expert"), None),
        P(("dp", "expert"), None),
        P(("dp", "expert"), None),
        P(("dp", "expert")),
        P(("dp", "expert")),
        P(),
        P("expert", None, "dp"),
        P("expert", "dp", None),
    )
    return jax.shard_map(shards, mesh=mesh, in_specs=in_specs, out_specs=out_specs, check_vma=False)
```

```python
import jax
import jax.numpy as jnp
import numpy as np
from jax import lax
from jax.sharding import PartitionSpec as P

EPS = 1e-06
MASKED = -1e30


def bucket_onehot(length, buckets):
    half_count = buckets // 2
    exact_count = half_count // 2
    offsets = np.arange(length)[None, :] - np.arange(length)[:, None]
    distance = np.abs(offsets)
    scaled = (
        np.log(np.maximum(distance, 1) / exact_count)
        / np.log(128.0 / exact_count)
        * (half_count - exact_count)
    )
    far_bucket = np.minimum(exact_count + np.floor(scaled).astype(np.int32), half_count - 1)
    bucket = np.where(distance < exact_count, distance, far_bucket) + np.where(
        offsets > 0, half_count, 0
    )
    return (bucket[:, :, None] == np.arange(buckets)[None, None, :]).astype(np.float32)


def rms_scale(values, gain_vec):
    return values * lax.rsqrt(jnp.mean(values * values, axis=-1, keepdims=True) + EPS) * gain_vec


def gelu_tanh(values):
    return jax.nn.gelu(values, approximate=True)


def left_dot(left, right):
    return lax.dot_general(
        left, right, (((0,), (0,)), ((), ())), preferred_element_type=jnp.float32
    )


def right_dot(left, right):
    return lax.dot_general(
        left, right, (((1,), (1,)), ((), ())), preferred_element_type=jnp.float32
    )


def two_terms(values):
    high = lax.reduce_precision(values, exponent_bits=8, mantissa_bits=7)
    return high.astype(jnp.bfloat16), (values - high).astype(jnp.bfloat16)


def shards(
    tokens,
    segments,
    routes,
    qkv_weight,
    out_weight,
    router_weight,
    attn_gain,
    moe_gain,
    bias_table,
    up_weight,
    down_weight,
    cotangent,
):
    micro_count, length = segments.shape
    rows, model_width = tokens.shape
    buckets, head_count = bias_table.shape
    head_size = model_width // head_count
    score_scale = head_size ** (-0.5)
    experts = router_weight.shape[1]
    capacity = max(2, (5 * length + 4 * experts - 1) // (4 * experts))
    packed_width = qkv_weight.shape[1]
    side_pad = (-(experts + 2)) % 128

    first_part = jnp.concatenate(
        [
            qkv_weight,
            router_weight,
            attn_gain[:, None],
            moe_gain[:, None],
            jnp.zeros((qkv_weight.shape[0], side_pad), jnp.bfloat16),
        ],
        axis=1,
    )
    own = jnp.concatenate([first_part, out_weight], axis=1)
    near = lax.all_to_all(
        jnp.broadcast_to(own[None], (lax.axis_size("expert"),) + own.shape),
        "expert",
        split_axis=0,
        concat_axis=0,
        tiled=True,
    ).reshape(-1, own.shape[1])
    first_width = first_part.shape[1]
    first_whole = lax.all_gather(near[:, :first_width], "dp", axis=0, tiled=True)
    w_out = lax.all_gather(near[:, first_width:], "dp", axis=0, tiled=True)
    w_qkv = first_whole[:, :packed_width]
    side = first_whole[:, packed_width:]
    w_router = side[:, :experts]
    gain_one = side[:, experts].astype(jnp.float32)
    gain_two = side[:, experts + 1].astype(jnp.float32)
    up_mat, down_mat = (up_weight[0], down_weight[0])

    bucket_hot = bucket_onehot(length, buckets)
    flat_hot = jnp.asarray(bucket_hot.reshape(length * length, buckets).astype(jnp.bfloat16))
    rel_bias = jnp.dot(flat_hot, bias_table, preferred_element_type=jnp.float32)
    rel_bias = rel_bias.reshape(length, length, head_count).transpose(2, 0, 1)

    inputs = tokens.astype(jnp.float32)
    upstream = cotangent.astype(jnp.float32)
    same_doc = segments[:, :, None] == segments[:, None, :]
    route_ids = routes[:, 0]
    route_hot = (route_ids[:, None] == jnp.arange(experts, dtype=jnp.int32)[None, :]).astype(
        jnp.float32
    )
    earlier = (
        (np.arange(rows)[:, None] > np.arange(rows)[None, :])
        & (np.arange(rows)[:, None] // length == np.arange(rows)[None, :] // length)
    ).astype(np.float32)
    same_route = route_ids[:, None] == route_ids[None, :]
    slot_index = jnp.sum(jnp.where(same_route, jnp.asarray(earlier), 0.0), axis=1).astype(jnp.int32)
    slab_index = jnp.arange(rows, dtype=jnp.int32) // length
    position = (route_ids * micro_count + slab_index) * capacity + slot_index
    slots = experts * micro_count * capacity
    dispatch = (jnp.arange(slots, dtype=jnp.int32)[:, None] == position[None, :]).astype(
        jnp.bfloat16
    )

    normed_one = rms_scale(inputs, gain_one).astype(jnp.bfloat16)
    packed = jnp.dot(normed_one, w_qkv, preferred_element_type=jnp.float32).astype(jnp.bfloat16)
    packed = packed.reshape(micro_count, length, 3, head_count, head_size)
    query_rows, key_rows, value_rows = (packed[:, :, 0], packed[:, :, 1], packed[:, :, 2])
    scores = (
        jnp.einsum("bqhd,bkhd->bhqk", query_rows, key_rows, preferred_element_type=jnp.float32)
        * score_scale
    )
    scores = jnp.where(same_doc[:, None], scores + rel_bias[None], MASKED)
    expo = jnp.exp(scores - jnp.max(scores, axis=-1, keepdims=True))
    attn_probs = expo / jnp.sum(expo, axis=-1, keepdims=True)
    probs_low = attn_probs.astype(jnp.bfloat16)
    attended = (
        jnp.einsum("bhqk,bkhd->bqhd", probs_low, value_rows, preferred_element_type=jnp.float32)
        .astype(jnp.bfloat16)
        .reshape(rows, model_width)
    )
    after_attn = inputs + jnp.dot(attended, w_out, preferred_element_type=jnp.float32)
    normed_two = rms_scale(after_attn, gain_two).astype(jnp.bfloat16)
    logits = jnp.dot(normed_two, w_router, preferred_element_type=jnp.float32)
    router_probs = jax.nn.softmax(logits, axis=-1)
    gate_prob = jnp.sum(router_probs * route_hot, axis=1, keepdims=True)
    grad_token_out = (gate_prob * upstream).astype(jnp.bfloat16)

    sent = jnp.dot(
        dispatch,
        jnp.concatenate([normed_two, grad_token_out], axis=1),
        preferred_element_type=jnp.float32,
    ).astype(jnp.bfloat16)
    received = lax.all_to_all(
        sent.reshape(experts, micro_count * capacity, 2 * model_width),
        "expert",
        split_axis=0,
        concat_axis=0,
        tiled=True,
    ).reshape(slots, 2 * model_width)
    expert_rows = lax.all_gather(received, "dp", axis=0, tiled=True)
    expert_in, grad_expert_out = (expert_rows[:, :model_width], expert_rows[:, model_width:])
    hidden = jnp.dot(expert_in, up_mat, preferred_element_type=jnp.float32)
    act, act_back = jax.vjp(gelu_tanh, hidden)
    act_low = act.astype(jnp.bfloat16)
    grad_activation = right_dot(grad_expert_out, down_mat)
    grad_hidden = act_back(grad_activation)[0].astype(jnp.bfloat16)
    results = jnp.concatenate(
        [
            jnp.dot(act_low, down_mat, preferred_element_type=jnp.float32).astype(jnp.bfloat16),
            right_dot(grad_hidden, up_mat).astype(jnp.bfloat16),
        ],
        axis=1,
    )
    results = lax.psum_scatter(results, "dp", scatter_dimension=0, tiled=True)
    returned = lax.all_to_all(
        results.reshape(experts, micro_count * capacity, 2 * model_width),
        "expert",
        split_axis=0,
        concat_axis=0,
        tiled=True,
    ).reshape(slots, 2 * model_width)
    acc_up = left_dot(expert_in, grad_hidden)
    acc_down = left_dot(act_low, grad_expert_out)
    back = left_dot(dispatch, returned)
    combined, grad_normed_two = (back[:, :model_width], back[:, model_width:])
    mixed = (after_attn + gate_prob * combined).astype(jnp.bfloat16)
    grad_gate = jnp.sum(upstream * combined, axis=1, keepdims=True)
    grad_logits = (router_probs * (route_hot - gate_prob) * grad_gate).astype(jnp.bfloat16)
    grad_normed_two = grad_normed_two + right_dot(grad_logits, w_router)
    grad_after_norm, grad_gain_two = jax.vjp(rms_scale, after_attn, gain_two)[1](grad_normed_two)
    grad_after = upstream + grad_after_norm
    grad_branch = grad_after.astype(jnp.bfloat16)

    acc_out = left_dot(attended, grad_branch)
    acc_router = left_dot(grad_logits, normed_two)
    out_near = lax.psum_scatter(
        acc_out.astype(jnp.bfloat16), "dp", scatter_dimension=0, tiled=True
    )

    grad_attended = (
        right_dot(grad_branch, w_out)
        .astype(jnp.bfloat16)
        .reshape(micro_count, length, head_count, head_size)
    )
    grad_value = jnp.einsum(
        "bhqk,bqhd->bkhd", probs_low, grad_attended, preferred_element_type=jnp.float32
    )
    grad_probs = jnp.einsum(
        "bqhd,bkhd->bhqk", grad_attended, value_rows, preferred_element_type=jnp.float32
    )
    grad_scores = attn_probs * (
        grad_probs - jnp.sum(attn_probs * grad_probs, axis=-1, keepdims=True)
    )
    scores_low = grad_scores.astype(jnp.bfloat16)
    grad_query = (
        jnp.einsum("bhqk,bkhd->bqhd", scores_low, key_rows, preferred_element_type=jnp.float32)
        * score_scale
    )
    grad_key = (
        jnp.einsum("bhqk,bqhd->bkhd", scores_low, query_rows, preferred_element_type=jnp.float32)
        * score_scale
    )
    grad_packed = (
        jnp.stack([grad_query, grad_key, grad_value], axis=2)
        .reshape(rows, packed_width)
        .astype(jnp.bfloat16)
    )
    grad_normed_one = right_dot(grad_packed, w_qkv)
    grad_input_norm, grad_gain_one = jax.vjp(rms_scale, inputs, gain_one)[1](grad_normed_one)
    grad_tokens = grad_after + grad_input_norm
    acc_qkv = left_dot(normed_one, grad_packed)
    qkv_sum, table_scores = lax.optimization_barrier(
        (acc_qkv.astype(jnp.bfloat16), jnp.sum(grad_scores, axis=0))
    )
    qkv_near = lax.psum_scatter(qkv_sum, "dp", scatter_dimension=0, tiled=True)

    high, low = two_terms(table_scores.reshape(head_count, length * length))
    table_parts = jnp.dot(
        jnp.concatenate([high, low], axis=0), flat_hot, preferred_element_type=jnp.float32
    )
    acc_table = (table_parts[:head_count] + table_parts[head_count:]).reshape(-1)

    shard_rows = qkv_weight.shape[0]
    experts_axis = near.shape[0] // shard_rows
    small_rows = experts + 3
    small = jnp.concatenate(
        [
            acc_router,
            grad_gain_one[None],
            grad_gain_two[None],
            jnp.pad(acc_table, (0, model_width - acc_table.shape[0]))[None],
            jnp.zeros(((-small_rows) % 8, model_width), jnp.float32),
        ],
        axis=0,
    )
    small = jnp.sum(lax.all_gather(small, "dp", axis=0, tiled=False), axis=0)
    mine = lax.dynamic_slice_in_dim(
        small[: experts + 2], lax.axis_index("dp") * near.shape[0], near.shape[0], axis=1
    )
    mine = mine.T.reshape(experts_axis, shard_rows, experts + 2)
    table_size = buckets * head_count
    table_columns = -(-table_size // shard_rows)
    table_block = jnp.pad(
        small[experts + 2, :table_size], (0, table_columns * shard_rows - table_size)
    ).reshape(1, shard_rows, table_columns)
    extra = jnp.concatenate(
        [mine, jnp.broadcast_to(table_block, (experts_axis, shard_rows, table_columns))], axis=2
    )
    extra_width = extra.shape[2]
    extra_high, extra_low = two_terms(extra)
    share = jnp.concatenate(
        [
            qkv_near.reshape(experts_axis, shard_rows, packed_width),
            out_near.reshape(experts_axis, shard_rows, model_width),
            extra_high,
            extra_low,
            jnp.zeros((experts_axis, shard_rows, (-2 * extra_width) % 128), jnp.bfloat16),
        ],
        axis=2,
    )
    share = lax.all_to_all(share, "expert", split_axis=0, concat_axis=0, tiled=True)
    share = jnp.sum(share.astype(jnp.float32), axis=0)
    dense_width = packed_width + model_width
    extra_sum = (
        share[:, dense_width : dense_width + extra_width]
        + share[:, dense_width + extra_width : dense_width + 2 * extra_width]
    )
    table_total = (
        extra_sum[:, experts + 2 :].reshape(-1)[:table_size].reshape(head_count, buckets).T
    )
    return (
        mixed,
        grad_tokens,
        share[:, :packed_width],
        share[:, packed_width:dense_width],
        extra_sum[:, :experts],
        extra_sum[:, experts],
        extra_sum[:, experts + 1],
        table_total,
        acc_up[None],
        acc_down[None],
    )


def solution(mesh):
    in_specs = (
        P(("dp", "expert"), None),
        P(("dp", "expert"), None),
        P(("dp", "expert"), None),
        P(("dp", "expert"), None),
        P(("dp", "expert"), None),
        P(("dp", "expert"), None),
        P(("dp", "expert")),
        P(("dp", "expert")),
        P(),
        P("expert", None, "dp"),
        P("expert", "dp", None),
        P(("dp", "expert"), None),
    )
    out_specs = (
        P(("dp", "expert"), None),
        P(("dp", "expert"), None),
        P(("dp", "expert"), None),
        P(("dp", "expert"), None),
        P(("dp", "expert"), None),
        P(("dp", "expert")),
        P(("dp", "expert")),
        P(),
        P("expert", None, "dp"),
        P("expert", "dp", None),
    )
    return jax.shard_map(shards, mesh=mesh, in_specs=in_specs, out_specs=out_specs, check_vma=False)
```
